512 devices in a mesh: island: 8 (over x, z_hi), fsdp: 8 (over z_lo), tensor: 8 (over y, core).
Axes of the slice: x: 4, y: 4, z: 16 (z_hi: 2, z_lo: 8; z = z_hi * 8 + z_lo), core: 2. Of those that a mesh axis runs over, the one named last changes fastest.
Arguments:
- x_saved: bfloat16 [8, 4096, 8192], P('island', 'fsdp', 'tensor'), may hold values from -6 to 6
- grad_keys: bfloat16 [8, 4096, 1024], P('island', 'fsdp'), may hold values from -0.09375 to 0.09375
- inner_weight: bfloat16 [8, 1024, 8192], P('island', 'fsdp', 'tensor'), may hold values from -0.0625 to 0.0625
- outer_weight: float32 [1024, 8, 8, 128], P('fsdp', 'tensor', 'island'), may hold values from -0.0625 to 0.0625
- outer_momentum: float32 [1024, 8, 8, 128], P('fsdp', 'tensor', 'island'), may hold values from -0.06 to 0.06
- x_next: bfloat16 [8, 4096, 8192], P('island', 'fsdp', 'tensor'), may hold values from -250 to 250
- norm_gain: float32 [8192], P('tensor'), may hold values from 0.1 to 1.9
Outputs:
- keys_next: bfloat16 [8, 4096, 1024], P('island', 'fsdp', 'tensor')
The draws below stay inside these ranges and needn't reach their ends.
All inputs are finite; a program needn't handle non-finite values.
Results may differ from the reference program's by a relative error of at most 0.029.
Values may be sent and summed in bfloat16 or wider, within the bound.
No kernel may reach another device: no remote copies, remote signals or barrier semaphores. Data moves between devices by JAX's collectives and lax.ppermute only.
A program may use at most 64 MiB of HBM per device.

```python
import math
import jax
import jax.numpy as jnp
from jax import lax

D = 8192
KVW = 1024
TOK_DEV = 512
TOKENS = 4096
R = 128
N_ISLAND = 8
N_FSDP = 8
N_TENSOR = 8


def draw_x_next(key, part):
    key = jax.random.fold_in(key, 11)
    first, second = jax.random.split(key, 2)
    position = jnp.arange(D, dtype=jnp.float32) / D
    base = jnp.clip(jax.random.normal(first, (N_ISLAND, TOKENS, D), jnp.float32), -5.0, 5.0)
    rows = jnp.exp(jax.random.uniform(second, (N_ISLAND, TOKENS, 1), jnp.float32, 0.0, math.log(10.0)))
    columns = jnp.exp(position * math.log(3.0))
    return (base * rows * columns[None, None, :]).astype(jnp.bfloat16)


def level_of(own_key, extent, shards, least, largest):
    loudness, own = 1.0, jax.random.fold_in(own_key, 6)
    for dim, parts in shards:
        heights = jnp.exp(jax.random.uniform(jax.random.fold_in(own, dim), (parts,), jnp.float32, least / len(shards), largest / len(shards)))
        loudness = loudness * jnp.repeat(heights, extent[dim] // parts).reshape([-1 if axis == dim else 1 for axis in range(len(extent))])
    return loudness


def scatter_about(rng, shape, scale, limit, shards=(), kind=jnp.bfloat16):
    array = scale * jax.random.normal(rng, shape, jnp.float32)
    if shards:
        array = array * level_of(rng, shape, shards, -0.22, 0.18)
    return jnp.clip(array, -limit, limit).astype(kind)


def setup_inputs(seed: int = 0) -> dict:
    splits = jax.random.split(jax.random.key(seed), 8)
    return {
        "x_saved": scatter_about(splits[0], (N_ISLAND, TOKENS, D), 1.0, 6.0, ((0, 8), (1, 8), (2, 8))),
        "grad_keys": scatter_about(splits[1], (N_ISLAND, TOKENS, KVW), TOKENS ** -0.5, 0.09375, ((0, 8), (1, 8))),
        "inner_weight": scatter_about(splits[2], (N_ISLAND, KVW, D), D ** -0.5, 0.0625, ((0, 8), (1, 8), (2, 8))),
        "outer_weight": scatter_about(splits[3], (KVW, N_TENSOR, N_ISLAND, R), D ** -0.5, 0.0625, ((0, 8), (1, 8), (2, 8)), jnp.float32),
        "outer_momentum": scatter_about(splits[4], (KVW, N_TENSOR, N_ISLAND, R), 0.01, 0.06, ((0, 8), (1, 8), (2, 8)), jnp.float32),
        "x_next": draw_x_next(jax.random.fold_in(splits[7], 71), 0),
        "norm_gain": jnp.clip(1.0 + 0.18 * jax.random.normal(splits[6], (D,), jnp.float32), 0.1, 1.9),
    }


def replica_gradient(pair):
    saved, cot = pair
    saved = saved.reshape(N_FSDP, TOK_DEV, D)
    cot = cot.reshape(N_FSDP, TOK_DEV, KVW)

    def add_block(total, block):
        term = lax.dot_general(block[1], block[0], (((0,), (0,)), ((), ())), preferred_element_type=jnp.float32)
        term = lax.optimization_barrier(term.astype(jnp.bfloat16))
        return (total + term.astype(jnp.float32), None)
    total, _ = lax.scan(add_block, jnp.zeros((KVW, D), jnp.float32), (saved, cot))
    return total

def replica_keys(normed, weight_blocks):
    blocks = normed.reshape(TOKENS, N_TENSOR, D // N_TENSOR).transpose(1, 0, 2)

    def add_block(total, block):
        part = lax.dot_general(block[0], block[1], (((1,), (1,)), ((), ())), preferred_element_type=jnp.float32)
        part = lax.optimization_barrier(part.astype(jnp.bfloat16))
        return (total + part.astype(jnp.float32), None)
    total, _ = lax.scan(add_block, jnp.zeros((TOKENS, KVW), jnp.float32), (blocks, weight_blocks))
    return total.astype(jnp.bfloat16)

def reference(x_saved, grad_keys, inner_weight, outer_weight, outer_momentum, x_next, norm_gain):
    gradient = lax.map(replica_gradient, (x_saved, grad_keys))
    updated = inner_weight.astype(jnp.float32) - 0.03 * gradient
    theta = outer_weight.reshape(KVW, D)
    mean_delta = theta - lax.optimization_barrier(jnp.sum(updated, axis=0)) / N_ISLAND
    momentum = 0.9 * outer_momentum.reshape(KVW, D) + mean_delta
    theta_new = theta - 0.7 * (mean_delta + 0.9 * momentum)
    weight_next = theta_new.astype(jnp.bfloat16)
    weight_blocks = weight_next.reshape(KVW, N_TENSOR, D // N_TENSOR).transpose(1, 0, 2)
    raw = x_next.astype(jnp.float32)
    scale = lax.rsqrt(lax.optimization_barrier(jnp.mean(raw * raw, axis=2, keepdims=True)) + 1e-05)
    normed = (raw * scale * norm_gain[None, None, :]).astype(jnp.bfloat16)
    return lax.map(lambda rows: replica_keys(rows, weight_blocks), normed)
```

```python
import jax
import jax.numpy as jnp
from jax import lax
from jax.sharding import Mesh, PartitionSpec as P

D = 8192
ISLANDS = 8
AXES = ("x", "z3", "z2", "z1", "z0", "y", "c")
NEAR = ("x", "z0")
FAR = ("z3", "z2", "z1")
ISLAND = ("x", "z3")
FSDP = ("z2", "z1", "z0")
TENSOR = ("y", "c")
STEP = 0.7 * 1.9
F32, BF16 = jnp.float32, jnp.bfloat16


def exchange(blocks, axes):
    return lax.all_to_all(blocks, axes, 0, 0)


def total(blocks):
    return jnp.sum(blocks.astype(F32), axis=0)


def spread(block, axes):
    everywhere = jnp.broadcast_to(block[None], (8, *block.shape))
    return exchange(everywhere, axes).reshape(-1, block.shape[-1])


def per_device(x_saved, grad_keys, inner_weight, outer_weight, outer_momentum, x_next, norm_gain):
    rows, width = outer_weight.shape[0], outer_weight.shape[3]
    island, fsdp = lax.axis_index(ISLAND), lax.axis_index(FSDP)
    term = lax.dot_general(
        grad_keys[0], x_saved[0], (((0,), (0,)), ((), ())), preferred_element_type=F32
    )
    share = STEP / ISLANDS
    theta = outer_weight.reshape(rows, width)
    momentum = outer_momentum.reshape(rows, width)
    own = (1.0 - STEP) * theta - 0.7 * 0.9 * 0.9 * momentum
    band = share * inner_weight[0].astype(F32)
    place = island * width
    band = lax.dynamic_update_slice(
        band, lax.dynamic_slice(band, (0, place), (rows, width)) + own, (0, place)
    )
    term = (-0.03 * share) * term
    start = fsdp * rows
    term = lax.dynamic_update_slice(
        term, lax.dynamic_slice(term, (start, 0), band.shape) + band, (start, 0)
    )
    features = term.shape[1]
    sums = total(exchange(term.astype(BF16).reshape(8, -1, features), NEAR)).astype(BF16)
    fresh = total(exchange(sums.reshape(8, -1, features), FAR)).astype(BF16)
    weight = spread(spread(fresh, FAR), NEAR)

    raw = x_next[0].astype(F32)
    squares = total(lax.all_gather(jnp.sum(raw * raw, axis=1), TENSOR, axis=0))
    scale = lax.rsqrt(squares / D + 1e-05)
    gained = (raw * norm_gain[None, :]).astype(BF16)
    partial = lax.dot_general(
        weight, gained, (((1,), (1,)), ((), ())), preferred_element_type=F32
    )
    tokens = partial.shape[1]
    keys = total(exchange(partial.astype(BF16).reshape(8, -1, tokens), TENSOR))
    return (keys * scale[None, :]).T.astype(BF16)[None]


def solution(mesh):
    fine = Mesh(mesh.devices.reshape(4, 2, 2, 2, 2, 4, 2), AXES)
    placed = (
        P(ISLAND, FSDP, TENSOR),
        P(ISLAND, FSDP, None),
        P(ISLAND, FSDP, TENSOR),
        P(FSDP, TENSOR, ISLAND, None),
        P(FSDP, TENSOR, ISLAND, None),
        P(ISLAND, FSDP, TENSOR),
        P(TENSOR),
    )
    return jax.shard_map(
        per_device,
        mesh=fine,
        in_specs=placed,
        out_specs=P(ISLAND, FSDP, TENSOR),
        check_vma=False,
    )
```

```python
import jax
import jax.numpy as jnp
from jax import lax
from jax.experimental import pallas as pl
from jax.experimental.pallas import tpu as pltpu
from jax.sharding import Mesh, PartitionSpec as P

D = 8192
ISLANDS = 8
R = 128
AXES = ("x", "z3", "z2", "z1", "z0", "y", "c")
NEAR = ("x", "z0")
FAR = ("z3", "z2", "z1")
ISLAND = ("x", "z3")
FSDP = ("z2", "z1", "z0")
TENSOR = ("y", "c")
STEP = 0.7 * 1.9
SHARE = STEP / ISLANDS
F32, BF16 = jnp.float32, jnp.bfloat16


def exchange(blocks, axes):
    return lax.all_to_all(blocks, axes, 0, 0)


def total(blocks):
    return jnp.sum(blocks.astype(F32), axis=0)


def project_kernel(x_ref, w_ref, out_ref, acc_ref, squares_ref):
    step = pl.program_id(0)

    @pl.when(step == 0)
    def _():
        acc_ref[...] = jnp.zeros_like(acc_ref)
        squares_ref[...] = jnp.zeros_like(squares_ref)

    x = x_ref[0]
    weight = w_ref[...].reshape(-1, R)
    acc_ref[...] += jnp.dot(x, weight, preferred_element_type=F32)
    squares = squares_ref[...]
    for j in range(x.shape[1] // R):
        part = x[:, j * R : (j + 1) * R].astype(F32)
        squares += part * part
    squares_ref[...] = squares

    @pl.when(step == pl.num_programs(0) - 1)
    def _():
        mean = jnp.sum(squares_ref[...], axis=1, keepdims=True) / D
        out_ref[...] = (acc_ref[...] * lax.rsqrt(mean + 1e-05)).astype(BF16)


def project(x_all, weight):
    blocks, tokens, features = x_all.shape
    return pl.pallas_call(
        project_kernel,
        grid=(blocks,),
        in_specs=[
            pl.BlockSpec((1, tokens, features), lambda s: (s, 0, 0)),
            pl.BlockSpec((8, 1, R, R), lambda s: (0, s, 0, 0)),
        ],
        out_specs=pl.BlockSpec((tokens, R), lambda s: (0, 0)),
        out_shape=jax.ShapeDtypeStruct((tokens, R), BF16),
        scratch_shapes=[pltpu.VMEM((tokens, R), F32), pltpu.VMEM((tokens, R), F32)],
        compiler_params=pltpu.CompilerParams(vmem_limit_bytes=24 * 2**20),
        cost_estimate=pl.CostEstimate(
            flops=2 * blocks * tokens * features * R,
            bytes_accessed=2 * blocks * (tokens * features + features * R),
            transcendentals=tokens,
        ),
    )(x_all, weight)


def per_device(x_saved, grad_keys, inner_weight, outer_weight, outer_momentum, x_next, norm_gain):
    rows, width = outer_weight.shape[0], outer_weight.shape[3]
    island, fsdp = lax.axis_index(ISLAND), lax.axis_index(FSDP)
    x_all = lax.all_gather(x_next[0], TENSOR, axis=0)

    term = lax.dot_general(
        x_saved[0], grad_keys[0], (((0,), (0,)), ((), ())), preferred_element_type=F32
    )
    theta = outer_weight.reshape(rows, width)
    momentum = outer_momentum.reshape(rows, width)
    own = (1.0 - STEP) * theta - 0.7 * 0.9 * 0.9 * momentum
    band = SHARE * inner_weight[0].astype(F32)
    place = island * width
    band = lax.dynamic_update_slice(
        band, lax.dynamic_slice(band, (0, place), (rows, width)) + own, (0, place)
    )
    band = band.T
    term = (-0.03 * SHARE) * term
    start = fsdp * rows
    term = lax.dynamic_update_slice(
        term, lax.dynamic_slice(term, (0, start), band.shape) + band, (0, start)
    )
    term = (term * norm_gain[:, None]).astype(BF16)
    keys = term.shape[1]
    sums = total(exchange(term.reshape(8, -1, keys), NEAR)).astype(BF16)
    fresh = total(exchange(sums.reshape(8, -1, keys), FAR)).astype(BF16)
    depth = fresh.shape[0]
    pieces = fresh.reshape(depth, 8, R).transpose(1, 0, 2)
    pieces = jnp.broadcast_to(pieces[:, None], (8, 8, depth, R)).reshape(64, depth, R)
    mine = exchange(pieces, TENSOR + FAR).reshape(8, 8 * depth, R)
    mine, x_all = lax.optimization_barrier((mine, x_all))
    weight = exchange(jnp.broadcast_to(mine[None], (8, *mine.shape)), NEAR)
    return project(x_all, weight)[None]


def solution(mesh):
    fine = Mesh(mesh.devices.reshape(4, 2, 2, 2, 2, 4, 2), AXES)
    placed = (
        P(ISLAND, FSDP, TENSOR),
        P(ISLAND, FSDP, None),
        P(ISLAND, FSDP, TENSOR),
        P(FSDP, TENSOR, ISLAND, None),
        P(FSDP, TENSOR, ISLAND, None),
        P(ISLAND, FSDP, TENSOR),
        P(TENSOR),
    )
    return jax.shard_map(
        per_device,
        mesh=fine,
        in_specs=placed,
        out_specs=P(ISLAND, FSDP, TENSOR),
        check_vma=False,
    )
```

```python
import jax
import jax.numpy as jnp
from jax import lax
from jax.experimental import pallas as pl
from jax.experimental.pallas import tpu as pltpu
from jax.sharding import Mesh, PartitionSpec as P

D = 8192
ISLANDS = 8
R = 128
AXES = ("x", "z3", "z2", "z1", "z0", "y", "c")
NEAR = ("x", "z0")
FAR = ("z3", "z2", "z1")
ISLAND = ("x", "z3")
FSDP = ("z2", "z1", "z0")
TENSOR = ("y", "c")
STEP = 0.7 * 1.9
SHARE = STEP / ISLANDS
F32, BF16 = jnp.float32, jnp.bfloat16
VMEM = 16 * 2**20


def exchange(blocks, axes):
    return lax.all_to_all(blocks, axes, 0, 0)


def total(blocks):
    return jnp.sum(blocks.astype(F32), axis=0)


def share_kernel(place_ref, x_ref, g_ref, w_ref, theta_ref, momentum_ref, gain_ref, out_ref):
    step = pl.program_id(0)
    width = x_ref.shape[1]
    term = lax.dot_general(
        x_ref[...], g_ref[...], (((0,), (0,)), ((), ())), preferred_element_type=F32
    )
    own = (1.0 - STEP) * theta_ref[...] - 0.7 * 0.9 * 0.9 * momentum_ref[...]
    band = []
    for j in range(width // R):
        here = place_ref[0] == step * (width // R) + j
        band.append(SHARE * w_ref[:, j * R : (j + 1) * R].astype(F32) + jnp.where(here, own, 0.0))
    band = jnp.concatenate(band, axis=1).T
    gain = jnp.broadcast_to(gain_ref[...], (R, width)).T
    for j in range(out_ref.shape[1] // R):
        piece = (-0.03 * SHARE) * term[:, j * R : (j + 1) * R]
        piece += jnp.where(place_ref[1] == j, band, 0.0)
        out_ref[:, j * R : (j + 1) * R] = (piece * gain).astype(BF16)


def share(place, x, g, weight, theta, momentum, gain):
    tokens, features = x.shape
    keys = g.shape[1]
    width = 4 * R
    whole = lambda *shape: pl.BlockSpec(shape, lambda i: (0, 0))
    return pl.pallas_call(
        share_kernel,
        grid=(features // width,),
        in_specs=[
            pl.BlockSpec(memory_space=pltpu.SMEM),
            pl.BlockSpec((tokens, width), lambda i: (0, i)),
            whole(tokens, keys),
            pl.BlockSpec((R, width), lambda i: (0, i)),
            whole(R, R),
            whole(R, R),
            pl.BlockSpec((1, width), lambda i: (0, i)),
        ],
        out_specs=pl.BlockSpec((width, keys), lambda i: (i, 0)),
        out_shape=jax.ShapeDtypeStruct((features, keys), BF16),
        compiler_params=pltpu.CompilerParams(vmem_limit_bytes=60 * 2**20),
        cost_estimate=pl.CostEstimate(
            flops=2 * tokens * features * keys, bytes_accessed=6 * 2**20, transcendentals=0
        ),
    )(place, x, g, weight, theta, momentum, gain)


def scale_kernel(*refs):
    x_refs, out_ref, x_all, sems = refs[:8], *refs[8:]
    copies = [
        pltpu.make_async_copy(x_ref, x_all.at[block], sems.at[block])
        for block, x_ref in enumerate(x_refs)
    ]
    for copy in copies:
        copy.start()
    for copy in copies:
        copy.wait()

    @pl.loop(0, out_ref.shape[0] // 64)
    def _(i):
        rows = pl.ds(pl.multiple_of(i * 64, 64), 64)
        squares = jnp.zeros((64, R), F32)
        for block in range(8):
            for j in range(x_all.shape[2] // R):
                part = x_all[block, rows, j * R : (j + 1) * R].astype(F32)
                squares += part * part
        mean = jnp.sum(squares, axis=1, keepdims=True) / D
        out_ref[rows, :] = jnp.broadcast_to(lax.rsqrt(mean + 1e-05), (64, R))


def scales(blocks):
    tokens, features = blocks[0].shape
    vmem = pl.BlockSpec(memory_space=pltpu.VMEM)
    return pl.pallas_call(
        scale_kernel,
        in_specs=[pl.BlockSpec(memory_space=pl.ANY)] * 8,
        out_specs=(vmem, vmem),
        out_shape=(
            jax.ShapeDtypeStruct((tokens, R), F32),
            jax.ShapeDtypeStruct((8, tokens, features), BF16),
        ),
        scratch_shapes=[pltpu.SemaphoreType.DMA((8,))],
        compiler_params=pltpu.CompilerParams(vmem_limit_bytes=VMEM),
        cost_estimate=pl.CostEstimate(
            flops=16 * tokens * features,
            bytes_accessed=32 * tokens * features,
            transcendentals=tokens,
        ),
    )(*blocks)


def project_kernel(own_ref, scale_ref, w_ref, x_ref, out_ref):
    acc = jnp.zeros(out_ref.shape, F32)
    for block in range(8):
        weight = w_ref[:, pl.ds(own_ref[0] ^ block, 1)].reshape(-1, R)
        acc += jnp.dot(x_ref[block], weight, preferred_element_type=F32)
    out_ref[...] = (acc * scale_ref[...]).astype(BF16)


def project(own, scale, weight, x_all):
    tokens, features = x_all.shape[1:]
    vmem = pl.BlockSpec(memory_space=pltpu.VMEM)
    return pl.pallas_call(
        project_kernel,
        in_specs=[pl.BlockSpec(memory_space=pltpu.SMEM)] + [vmem] * 3,
        out_specs=vmem,
        out_shape=jax.ShapeDtypeStruct((tokens, R), BF16),
        compiler_params=pltpu.CompilerParams(vmem_limit_bytes=VMEM),
        cost_estimate=pl.CostEstimate(
            flops=16 * tokens * features * R,
            bytes_accessed=16 * (tokens * features + features * R),
            transcendentals=0,
        ),
    )(own, scale, weight, x_all)


def swap(block, bits):
    return lax.ppermute(block, TENSOR, [(t, t ^ bits) for t in range(8)])


def per_device(x_saved, grad_keys, inner_weight, outer_weight, outer_momentum, x_next, norm_gain):
    rows, width = outer_weight.shape[0], outer_weight.shape[3]
    place = jnp.stack([lax.axis_index(ISLAND), lax.axis_index(FSDP)]).astype(jnp.int32)
    term = share(
        place,
        x_saved[0],
        grad_keys[0],
        inner_weight[0],
        outer_weight.reshape(rows, width),
        outer_momentum.reshape(rows, width),
        norm_gain[None],
    )
    keys = term.shape[1]
    x_own = x_next[0]
    x_core, x_up, x_down, x_far = (swap(x_own, bits) for bits in (1, 2, 6, 4))
    sums = exchange(term.reshape(8, -1, keys), NEAR)
    sums, x_core = lax.optimization_barrier((sums, x_core))
    fresh = exchange(total(sums).astype(BF16).reshape(8, -1, keys), FAR)
    fresh, x_up, x_down, x_far = lax.optimization_barrier((fresh, x_up, x_down, x_far))
    fresh = total(fresh).astype(BF16)
    depth = fresh.shape[0]
    pieces = fresh.reshape(depth, 8, R).transpose(1, 0, 2)
    pieces = jnp.broadcast_to(pieces[:, None], (8, 8, depth, R)).reshape(64, depth, R)
    mine = exchange(pieces, TENSOR + FAR).reshape(8, 8 * depth, R)
    mine, x_up, x_down, x_far = lax.optimization_barrier((mine, x_up, x_down, x_far))
    x_up_core, x_down_core, x_far_core = swap(x_up, 1), swap(x_down, 1), swap(x_far, 1)
    blocks = (x_own, x_core, x_up, x_up_core, x_far, x_far_core, x_down, x_down_core)
    scale, x_all = scales(blocks)
    weight = exchange(jnp.broadcast_to(mine[None], (8, *mine.shape)), NEAR)
    own = lax.axis_index(TENSOR).astype(jnp.int32)[None]
    return project(own, scale, weight, x_all)[None]


def solution(mesh):
    fine = Mesh(mesh.devices.reshape(4, 2, 2, 2, 2, 4, 2), AXES)
    placed = (
        P(ISLAND, FSDP, TENSOR),
        P(ISLAND, FSDP, None),
        P(ISLAND, FSDP, TENSOR),
        P(FSDP, TENSOR, ISLAND, None),
        P(FSDP, TENSOR, ISLAND, None),
        P(ISLAND, FSDP, TENSOR),
        P(TENSOR),
    )
    return jax.shard_map(
        per_device,
        mesh=fine,
        in_specs=placed,
        out_specs=P(ISLAND, FSDP, TENSOR),
        check_vma=False,
    )
```

```python
import jax
import jax.numpy as jnp
from jax import lax
from jax.experimental import pallas as pl
from jax.experimental.pallas import tpu as pltpu
from jax.sharding import Mesh, PartitionSpec as P

D = 8192
ISLANDS = 8
R = 128
AXES = ("x", "z3", "z2", "z1", "z0", "y", "c")
NEAR = ("x", "z0")
FAR = ("z3", "z2", "z1")
ISLAND = ("x", "z3")
FSDP = ("z2", "z1", "z0")
TENSOR = ("y", "c")
STEP = 0.7 * 1.9
SHARE = STEP / ISLANDS
F32, BF16 = jnp.float32, jnp.bfloat16
VMEM = 16 * 2**20


def exchange(blocks, axes):
    return lax.all_to_all(blocks, axes, 0, 0)


def total(blocks):
    return jnp.sum(blocks.astype(F32), axis=0)


def share_kernel(place_ref, x_ref, g_ref, w_ref, theta_ref, momentum_ref, gain_ref, out_ref):
    step = pl.program_id(0)
    width = x_ref.shape[1]
    term = lax.dot_general(
        x_ref[...], g_ref[...], (((0,), (0,)), ((), ())), preferred_element_type=F32
    )
    own = (1.0 - STEP) * theta_ref[...] - 0.7 * 0.9 * 0.9 * momentum_ref[...]
    band = []
    for j in range(width // R):
        here = place_ref[0] == step * (width // R) + j
        band.append(SHARE * w_ref[:, j * R : (j + 1) * R].astype(F32) + jnp.where(here, own, 0.0))
    band = jnp.concatenate(band, axis=1).T
    gain = jnp.broadcast_to(gain_ref[...], (R, width)).T
    for j in range(out_ref.shape[1] // R):
        piece = (-0.03 * SHARE) * term[:, j * R : (j + 1) * R]
        piece += jnp.where(place_ref[1] == j, band, 0.0)
        out_ref[:, j * R : (j + 1) * R] = (piece * gain).astype(BF16)


def share(place, x, g, weight, theta, momentum, gain):
    tokens, features = x.shape
    keys = g.shape[1]
    width = 4 * R
    whole = lambda *shape: pl.BlockSpec(shape, lambda i: (0, 0))
    return pl.pallas_call(
        share_kernel,
        grid=(features // width,),
        in_specs=[
            pl.BlockSpec(memory_space=pltpu.SMEM),
            pl.BlockSpec((tokens, width), lambda i: (0, i)),
            whole(tokens, keys),
            pl.BlockSpec((R, width), lambda i: (0, i)),
            whole(R, R),
            whole(R, R),
            pl.BlockSpec((1, width), lambda i: (0, i)),
        ],
        out_specs=pl.BlockSpec((width, keys), lambda i: (i, 0)),
        out_shape=jax.ShapeDtypeStruct((features, keys), BF16),
        compiler_params=pltpu.CompilerParams(vmem_limit_bytes=60 * 2**20),
        cost_estimate=pl.CostEstimate(
            flops=2 * tokens * features * keys, bytes_accessed=6 * 2**20, transcendentals=0
        ),
    )(place, x, g, weight, theta, momentum, gain)


def project_kernel(place_ref, w_ref, *refs):
    x_refs, (keep_ref, squares_ref, send_ref) = refs[:4], refs[4:]
    tokens = keep_ref.shape[0]
    acc = jnp.zeros((tokens, 2 * R), F32)
    for block, x_ref in enumerate(x_refs):
        weight = w_ref[:, pl.ds(place_ref[2] ^ block, 1)].reshape(-1, 2 * R)
        acc += jnp.dot(x_ref[...], weight, preferred_element_type=F32)
    squares = jnp.zeros((tokens, R), F32)
    for x_ref in x_refs:
        for j in range(x_ref.shape[1] // R):
            part = x_ref[:, j * R : (j + 1) * R].astype(F32)
            squares += part * part
    squares = jnp.broadcast_to(jnp.sum(squares, axis=1, keepdims=True), (tokens, R))
    first = place_ref[3] == 0
    keep_ref[...] = jnp.where(first, acc[:, :R], acc[:, R:])
    squares_ref[...] = squares
    high = squares.astype(BF16)
    low = (squares - high.astype(F32)).astype(BF16)
    lane = lax.broadcasted_iota(jnp.int32, (tokens, R), 1)
    send_ref[:, :R] = jnp.where(first, acc[:, R:], acc[:, :R]).astype(BF16)
    send_ref[:, R:] = jnp.where(lane < R // 2, high.astype(F32), low.astype(F32)).astype(BF16)


def project(place, weight, blocks):
    tokens, features = blocks[0].shape
    vmem = pl.BlockSpec(memory_space=pltpu.VMEM)
    return pl.pallas_call(
        project_kernel,
        in_specs=[pl.BlockSpec(memory_space=pltpu.SMEM)] + [vmem] * 5,
        out_specs=(vmem,) * 3,
        out_shape=(
            jax.ShapeDtypeStruct((tokens, R), F32),
            jax.ShapeDtypeStruct((tokens, R), F32),
            jax.ShapeDtypeStruct((tokens, 2 * R), BF16),
        ),
        compiler_params=pltpu.CompilerParams(vmem_limit_bytes=VMEM),
        cost_estimate=pl.CostEstimate(
            flops=16 * tokens * features * R,
            bytes_accessed=8 * (tokens * features + 2 * features * R),
            transcendentals=0,
        ),
    )(place, weight, *blocks)


def finish_kernel(keep_ref, squares_ref, got_ref, out_ref):
    other = got_ref[:, R:].astype(F32)
    other = other[:, :1] + other[:, R // 2 : R // 2 + 1]
    scale = lax.rsqrt((squares_ref[...] + other) / D + 1e-05)
    out_ref[...] = ((keep_ref[...] + got_ref[:, :R].astype(F32)) * scale).astype(BF16)


def finish(keep, squares, got):
    vmem = pl.BlockSpec(memory_space=pltpu.VMEM)
    return pl.pallas_call(
        finish_kernel,
        in_specs=[vmem] * 3,
        out_specs=vmem,
        out_shape=jax.ShapeDtypeStruct(keep.shape, BF16),
        compiler_params=pltpu.CompilerParams(vmem_limit_bytes=VMEM),
    )(keep, squares, got)


def swap(block, bits):
    return lax.ppermute(block, TENSOR, [(t, t ^ bits) for t in range(8)])


def per_device(x_saved, grad_keys, inner_weight, outer_weight, outer_momentum, x_next, norm_gain):
    rows, width = outer_weight.shape[0], outer_weight.shape[3]
    place = jnp.stack([lax.axis_index(axis) for axis in (ISLAND, FSDP, "y", "c")])
    place = place.astype(jnp.int32)
    term = share(
        place,
        x_saved[0],
        grad_keys[0],
        inner_weight[0],
        outer_weight.reshape(rows, width),
        outer_momentum.reshape(rows, width),
        norm_gain[None],
    )
    keys = term.shape[1]
    x_own = x_next[0]
    x_up, x_down, x_far = (swap(x_own, bits) for bits in (2, 6, 4))
    sums = exchange(term.reshape(8, -1, keys), NEAR)
    fresh = exchange(total(sums).astype(BF16).reshape(8, -1, keys), FAR)
    fresh, x_up, x_down, x_far = lax.optimization_barrier((fresh, x_up, x_down, x_far))
    fresh = total(fresh).astype(BF16)
    depth = fresh.shape[0]
    pieces = fresh.reshape(depth, 4, 2 * R).transpose(1, 0, 2)
    pieces = jnp.broadcast_to(pieces[:, None], (4, 8, depth, 2 * R)).reshape(32, depth, 2 * R)
    mine = exchange(pieces, ("y",) + FAR).reshape(4, 8 * depth, 2 * R)
    weight = exchange(jnp.broadcast_to(mine[None], (8, *mine.shape)), NEAR)
    keep, squares, send = project(place, weight, (x_own, x_up, x_far, x_down))
    return finish(keep, squares, swap(send, 1))[None]


def solution(mesh):
    fine = Mesh(mesh.devices.reshape(4, 2, 2, 2, 2, 4, 2), AXES)
    placed = (
        P(ISLAND, FSDP, TENSOR),
        P(ISLAND, FSDP, None),
        P(ISLAND, FSDP, TENSOR),
        P(FSDP, TENSOR, ISLAND, None),
        P(FSDP, TENSOR, ISLAND, None),
        P(ISLAND, FSDP, TENSOR),
        P(TENSOR),
    )
    return jax.shard_map(
        per_device,
        mesh=fine,
        in_specs=placed,
        out_specs=P(ISLAND, FSDP, TENSOR),
        check_vma=False,
    )
```

```python
import jax
import jax.numpy as jnp
from jax import lax
from jax.experimental import pallas as pl
from jax.experimental.pallas import tpu as pltpu
from jax.sharding import Mesh, PartitionSpec as P

D = 8192
ISLANDS = 8
R = 128
AXES = ("x", "z3", "z2", "z1", "z0", "y", "c")
NEAR = ("x", "z0")
FAR = ("z3", "z2", "z1")
ISLAND = ("x", "z3")
FSDP = ("z2", "z1", "z0")
TENSOR = ("y", "c")
STEP = 0.7 * 1.9
SHARE = STEP / ISLANDS
F32, BF16 = jnp.float32, jnp.bfloat16
VMEM = 16 * 2**20


def exchange(blocks, axes):
    return lax.all_to_all(blocks, axes, 0, 0)


def total(blocks):
    return jnp.sum(blocks.astype(F32), axis=0)


def share_kernel(x_ref, g_ref, w_ref, theta_ref, momentum_ref, gain_ref, out_ref):
    step = pl.program_id(0)
    island, fsdp = lax.axis_index(ISLAND), lax.axis_index(FSDP)
    width = x_ref.shape[1]
    term = lax.dot_general(
        x_ref[...], g_ref[...], (((0,), (0,)), ((), ())), preferred_element_type=F32
    )
    own = (1.0 - STEP) * theta_ref[...] - 0.7 * 0.9 * 0.9 * momentum_ref[...]
    band = []
    for j in range(width // R):
        here = island == step * (width // R) + j
        band.append(SHARE * w_ref[:, j * R : (j + 1) * R].astype(F32) + jnp.where(here, own, 0.0))
    band = jnp.concatenate(band, axis=1).T
    gain = jnp.broadcast_to(gain_ref[...], (R, width)).T
    for j in range(out_ref.shape[1] // R):
        piece = (-0.03 * SHARE) * term[:, j * R : (j + 1) * R]
        piece += jnp.where(fsdp == j, band, 0.0)
        out_ref[:, j * R : (j + 1) * R] = (piece * gain).astype(BF16)


def share(x, g, weight, theta, momentum, gain):
    tokens, features = x.shape
    keys = g.shape[1]
    width = 4 * R
    whole = lambda *shape: pl.BlockSpec(shape, lambda i: (0, 0))
    return pl.pallas_call(
        share_kernel,
        grid=(features // width,),
        in_specs=[
            pl.BlockSpec((tokens, width), lambda i: (0, i)),
            whole(tokens, keys),
            pl.BlockSpec((R, width), lambda i: (0, i)),
            whole(R, R),
            whole(R, R),
            pl.BlockSpec((1, width), lambda i: (0, i)),
        ],
        out_specs=pl.BlockSpec((width, keys), lambda i: (i, 0)),
        out_shape=jax.ShapeDtypeStruct((features, keys), BF16),
        compiler_params=pltpu.CompilerParams(vmem_limit_bytes=60 * 2**20),
        cost_estimate=pl.CostEstimate(
            flops=2 * tokens * features * keys, bytes_accessed=6 * 2**20, transcendentals=0
        ),
    )(x, g, weight, theta, momentum, gain)


def total_kernel(blocks_ref, out_ref, vmem_ref, sems):
    parts, size = 4, out_ref.shape[1] // 4
    copies = []
    for part in range(parts):
        rows = pl.ds(part * size, size)
        copies.append(
            pltpu.make_async_copy(blocks_ref.at[:, rows], vmem_ref.at[:, rows], sems.at[part])
        )
        copies[-1].start()
    for part in range(parts):
        copies[part].wait()
        rows = slice(part * size, (part + 1) * size)
        block = jnp.sum(vmem_ref[:, rows].astype(F32), axis=0).astype(BF16)
        for j in range(4):
            out_ref[j, rows] = block[:, j * 2 * R : (j + 1) * 2 * R]


def total_far(blocks):
    return pl.pallas_call(
        total_kernel,
        in_specs=[pl.BlockSpec(memory_space=pl.ANY)],
        out_specs=pl.BlockSpec(memory_space=pltpu.VMEM),
        out_shape=jax.ShapeDtypeStruct((4, blocks.shape[1], 2 * R), BF16),
        scratch_shapes=[pltpu.VMEM(blocks.shape, BF16), pltpu.SemaphoreType.DMA((4,))],
        compiler_params=pltpu.CompilerParams(vmem_limit_bytes=VMEM),
        cost_estimate=pl.CostEstimate(
            flops=blocks.size, bytes_accessed=3 * blocks.size, transcendentals=0
        ),
    )(blocks)


def project_kernel(w_ref, *refs):
    x_refs, (keep_ref, squares_ref, send_ref) = refs[:4], refs[4:]
    own, core = lax.axis_index("y"), lax.axis_index("c")
    tokens = keep_ref.shape[0]
    acc = jnp.zeros((tokens, 2 * R), F32)
    for block, x_ref in enumerate(x_refs):
        acc += jnp.dot(x_ref[...], w_ref[:, :, pl.ds(own ^ block, 1)].reshape(-1, 2 * R), preferred_element_type=F32)
    squares = jnp.zeros((tokens, R), F32)
    for x_ref in x_refs:
        for j in range(x_ref.shape[1] // R):
            part = x_ref[:, j * R : (j + 1) * R].astype(F32)
            squares += part * part
    squares = jnp.broadcast_to(jnp.sum(squares, axis=1, keepdims=True), (tokens, R))
    first = core == 0
    keep_ref[...] = jnp.where(first, acc[:, :R], acc[:, R:])
    squares_ref[...] = squares
    high = squares.astype(BF16)
    low = (squares - high.astype(F32)).astype(BF16)
    lane = lax.broadcasted_iota(jnp.int32, (tokens, R), 1)
    send_ref[:, :R] = jnp.where(first, acc[:, R:], acc[:, :R]).astype(BF16)
    send_ref[:, R:] = jnp.where(lane < R // 2, high.astype(F32), low.astype(F32)).astype(BF16)


def project(weight, blocks):
    tokens, features = blocks[0].shape
    vmem = pl.BlockSpec(memory_space=pltpu.VMEM)
    return pl.pallas_call(
        project_kernel,
        in_specs=[vmem] * 5,
        out_specs=(vmem,) * 3,
        out_shape=(
            jax.ShapeDtypeStruct((tokens, R), F32),
            jax.ShapeDtypeStruct((tokens, R), F32),
            jax.ShapeDtypeStruct((tokens, 2 * R), BF16),
        ),
        compiler_params=pltpu.CompilerParams(vmem_limit_bytes=VMEM),
        cost_estimate=pl.CostEstimate(
            flops=16 * tokens * features * R,
            bytes_accessed=8 * (tokens * features + 2 * features * R),
            transcendentals=0,
        ),
    )(weight, *blocks)


def finish_kernel(keep_ref, squares_ref, got_ref, out_ref):
    other = got_ref[:, R:].astype(F32)
    other = other[:, :1] + other[:, R // 2 : R // 2 + 1]
    scale = lax.rsqrt((squares_ref[...] + other) / D + 1e-05)
    out_ref[...] = ((keep_ref[...] + got_ref[:, :R].astype(F32)) * scale).astype(BF16)


def finish(keep, squares, got):
    vmem = pl.BlockSpec(memory_space=pltpu.VMEM)
    return pl.pallas_call(
        finish_kernel,
        in_specs=[vmem] * 3,
        out_specs=vmem,
        out_shape=jax.ShapeDtypeStruct(keep.shape, BF16),
        compiler_params=pltpu.CompilerParams(vmem_limit_bytes=VMEM),
    )(keep, squares, got)


def swap(block, bits):
    return lax.ppermute(block, TENSOR, [(t, t ^ bits) for t in range(8)])


def per_device(x_saved, grad_keys, inner_weight, outer_weight, outer_momentum, x_next, norm_gain):
    rows, width = outer_weight.shape[0], outer_weight.shape[3]
    term = share(
        x_saved[0],
        grad_keys[0],
        inner_weight[0],
        outer_weight.reshape(rows, width),
        outer_momentum.reshape(rows, width),
        norm_gain[None],
    )
    keys = term.shape[1]
    x_own = x_next[0]
    x_up, x_down, x_far = (swap(x_own, bits) for bits in (2, 6, 4))
    sums = exchange(term.reshape(8, -1, keys), NEAR)
    fresh = exchange(total_far(sums).reshape(32, -1, 2 * R), ("y",) + FAR)
    fresh, x_up, x_down = lax.optimization_barrier((fresh, x_up, x_down))
    fresh = jnp.sum(fresh.reshape(4, 8, -1, 2 * R).astype(F32), axis=1).astype(BF16)
    mine = exchange(jnp.broadcast_to(fresh[None], (8, *fresh.shape)), FAR)
    mine, x_far = lax.optimization_barrier((mine, x_far))
    mine = mine.reshape(-1, 2 * R)
    weight = exchange(jnp.broadcast_to(mine[None], (8, *mine.shape)), NEAR)
    weight = weight.reshape(8, 8, 4, -1, 2 * R)
    keep, squares, send = project(weight, (x_own, x_up, x_far, x_down))
    return finish(keep, squares, swap(send, 1))[None]


def solution(mesh):
    fine = Mesh(mesh.devices.reshape(4, 2, 2, 2, 2, 4, 2), AXES)
    placed = (
        P(ISLAND, FSDP, TENSOR),
        P(ISLAND, FSDP, None),
        P(ISLAND, FSDP, TENSOR),
        P(FSDP, TENSOR, ISLAND, None),
        P(FSDP, TENSOR, ISLAND, None),
        P(ISLAND, FSDP, TENSOR),
        P(TENSOR),
    )
    return jax.shard_map(
        per_device,
        mesh=fine,
        in_specs=placed,
        out_specs=P(ISLAND, FSDP, TENSOR),
        check_vma=False,
    )
```

```python
import jax
import jax.numpy as jnp
from jax import lax
from jax.experimental import pallas as pl
from jax.experimental.pallas import tpu as pltpu
from jax.sharding import Mesh, PartitionSpec as P

D = 8192
ISLANDS = 8
R = 128
AXES = ("x", "z3", "z2", "z1", "z0", "y", "c")
NEAR = ("x", "z0")
FAR = ("z3", "z2", "z1")
ISLAND = ("x", "z3")
FSDP = ("z2", "z1", "z0")
TENSOR = ("y", "c")
STEP = 0.7 * 1.9
SHARE = STEP / ISLANDS
F32, BF16 = jnp.float32, jnp.bfloat16
VMEM = 16 * 2**20


def exchange(blocks, axes):
    return lax.all_to_all(blocks, axes, 0, 0)


def total(blocks):
    return jnp.sum(blocks.astype(F32), axis=0)


def share_kernel(x_ref, g_ref, w_ref, theta_ref, momentum_ref, gain_ref, out_ref):
    step = pl.program_id(0)
    island, fsdp = lax.axis_index(ISLAND), lax.axis_index(FSDP)
    width = x_ref.shape[1]
    term = lax.dot_general(
        x_ref[...], g_ref[...], (((0,), (0,)), ((), ())), preferred_element_type=F32
    )
    own = (1.0 - STEP) * theta_ref[...] - 0.7 * 0.9 * 0.9 * momentum_ref[...]
    band = []
    for j in range(width // R):
        here = island == step * (width // R) + j
        band.append(SHARE * w_ref[:, j * R : (j + 1) * R].astype(F32) + jnp.where(here, own, 0.0))
    band = jnp.concatenate(band, axis=1).T
    gain = jnp.broadcast_to(gain_ref[...], (R, width)).T
    for j in range(out_ref.shape[1] // R):
        piece = (-0.03 * SHARE) * term[:, j * R : (j + 1) * R]
        piece += jnp.where(fsdp == j, band, 0.0)
        out_ref[:, j * R : (j + 1) * R] = (piece * gain).astype(BF16)


def share(x, g, weight, theta, momentum, gain):
    tokens, features = x.shape
    keys = g.shape[1]
    width = 4 * R
    whole = lambda *shape: pl.BlockSpec(shape, lambda i: (0, 0))
    return pl.pallas_call(
        share_kernel,
        grid=(features // width,),
        in_specs=[
            pl.BlockSpec((tokens, width), lambda i: (0, i)),
            whole(tokens, keys),
            pl.BlockSpec((R, width), lambda i: (0, i)),
            whole(R, R),
            whole(R, R),
            pl.BlockSpec((1, width), lambda i: (0, i)),
        ],
        out_specs=pl.BlockSpec((width, keys), lambda i: (i, 0)),
        out_shape=jax.ShapeDtypeStruct((features, keys), BF16),
        compiler_params=pltpu.CompilerParams(vmem_limit_bytes=60 * 2**20),
        cost_estimate=pl.CostEstimate(
            flops=2 * tokens * features * keys, bytes_accessed=6 * 2**20, transcendentals=0
        ),
    )(x, g, weight, theta, momentum, gain)


def total_kernel(blocks_ref, out_ref, vmem_ref, sems):
    parts, size = 4, out_ref.shape[0] * 4
    copies = []
    for part in range(parts):
        rows = pl.ds(part * size, size)
        copies.append(
            pltpu.make_async_copy(blocks_ref.at[:, rows], vmem_ref.at[:, rows], sems.at[part])
        )
        copies[-1].start()
    for part in range(parts):
        copies[part].wait()
        rows = slice(part * size, (part + 1) * size)
        block = jnp.sum(vmem_ref[:, rows].astype(F32), axis=0).astype(BF16)
        for i in range(size // 16):
            for j in range(4):
                piece = block[i * 16 : (i + 1) * 16, j * 2 * R : (j + 1) * 2 * R]
                out_ref[part * (size // 16) + i, j] = piece


def total_far(blocks):
    return pl.pallas_call(
        total_kernel,
        in_specs=[pl.BlockSpec(memory_space=pl.ANY)],
        out_specs=pl.BlockSpec(memory_space=pltpu.VMEM),
        out_shape=jax.ShapeDtypeStruct((blocks.shape[1] // 16, 4, 16, 2 * R), BF16),
        scratch_shapes=[pltpu.VMEM(blocks.shape, BF16), pltpu.SemaphoreType.DMA((4,))],
        compiler_params=pltpu.CompilerParams(vmem_limit_bytes=VMEM),
        cost_estimate=pl.CostEstimate(
            flops=blocks.size, bytes_accessed=3 * blocks.size, transcendentals=0
        ),
    )(blocks)


def squares_kernel(*refs):
    x_refs, out_ref = refs[:4], refs[4]

    @pl.loop(0, out_ref.shape[0] // 64)
    def _(i):
        rows = pl.ds(pl.multiple_of(i * 64, 64), 64)
        squares = jnp.zeros((64, R), F32)
        for x_ref in x_refs:
            for j in range(x_ref.shape[1] // R):
                part = x_ref[rows, j * R : (j + 1) * R].astype(F32)
                squares += part * part
        out_ref[rows, :] = jnp.broadcast_to(jnp.sum(squares, axis=1, keepdims=True), (64, R))


def squares_of(blocks):
    tokens, features = blocks[0].shape
    vmem = pl.BlockSpec(memory_space=pltpu.VMEM)
    return pl.pallas_call(
        squares_kernel,
        in_specs=[vmem] * 4,
        out_specs=vmem,
        out_shape=jax.ShapeDtypeStruct((tokens, R), F32),
        compiler_params=pltpu.CompilerParams(vmem_limit_bytes=VMEM),
        cost_estimate=pl.CostEstimate(
            flops=8 * tokens * features, bytes_accessed=8 * tokens * features, transcendentals=0
        ),
    )(*blocks)


def project_kernel(w_ref, squares_ref, *refs):
    x_refs, (keep_ref, send_ref) = refs[:4], refs[4:]
    squares = squares_ref[...]
    own, core = lax.axis_index("y"), lax.axis_index("c")
    tokens = keep_ref.shape[0]
    acc = jnp.zeros((tokens, 2 * R), F32)
    for block, x_ref in enumerate(x_refs):
        acc += jnp.dot(x_ref[...], w_ref[:, :, pl.ds(own ^ block, 1)].reshape(-1, 2 * R), preferred_element_type=F32)
    first = core == 0
    keep_ref[...] = jnp.where(first, acc[:, :R], acc[:, R:])
    high = squares.astype(BF16)
    low = (squares - high.astype(F32)).astype(BF16)
    lane = lax.broadcasted_iota(jnp.int32, (tokens, R), 1)
    send_ref[:, :R] = jnp.where(first, acc[:, R:], acc[:, :R]).astype(BF16)
    send_ref[:, R:] = jnp.where(lane < R // 2, high.astype(F32), low.astype(F32)).astype(BF16)


def project(weight, squares, blocks):
    tokens, features = blocks[0].shape
    vmem = pl.BlockSpec(memory_space=pltpu.VMEM)
    return pl.pallas_call(
        project_kernel,
        in_specs=[vmem] * 6,
        out_specs=(vmem,) * 2,
        out_shape=(
            jax.ShapeDtypeStruct((tokens, R), F32),
            jax.ShapeDtypeStruct((tokens, 2 * R), BF16),
        ),
        compiler_params=pltpu.CompilerParams(vmem_limit_bytes=VMEM),
        cost_estimate=pl.CostEstimate(
            flops=16 * tokens * features * R,
            bytes_accessed=8 * (tokens * features + 2 * features * R),
            transcendentals=0,
        ),
    )(weight, squares, *blocks)


def finish_kernel(keep_ref, squares_ref, got_ref, out_ref):
    other = got_ref[:, R:].astype(F32)
    other = other[:, :1] + other[:, R // 2 : R // 2 + 1]
    scale = lax.rsqrt((squares_ref[...] + other) / D + 1e-05)
    out_ref[...] = ((keep_ref[...] + got_ref[:, :R].astype(F32)) * scale).astype(BF16)


def finish(keep, squares, got):
    vmem = pl.BlockSpec(memory_space=pltpu.VMEM)
    return pl.pallas_call(
        finish_kernel,
        in_specs=[vmem] * 3,
        out_specs=vmem,
        out_shape=jax.ShapeDtypeStruct(keep.shape, BF16),
        compiler_params=pltpu.CompilerParams(vmem_limit_bytes=VMEM),
    )(keep, squares, got)


def swap(block, bits):
    return lax.ppermute(block, TENSOR, [(t, t ^ bits) for t in range(8)])


def per_device(x_saved, grad_keys, inner_weight, outer_weight, outer_momentum, x_next, norm_gain):
    rows, width = outer_weight.shape[0], outer_weight.shape[3]
    term = share(
        x_saved[0],
        grad_keys[0],
        inner_weight[0],
        outer_weight.reshape(rows, width),
        outer_momentum.reshape(rows, width),
        norm_gain[None],
    )
    keys = term.shape[1]
    x_own = x_next[0]
    x_up, x_down, x_far = (swap(x_own, bits) for bits in (2, 6, 4))
    sums = exchange(term.reshape(8, -1, keys), NEAR)
    fresh = exchange(total_far(sums).reshape(32, -1, 2 * R), FAR + ("y",))
    fresh, x_up, x_down = lax.optimization_barrier((fresh, x_up, x_down))
    fresh = jnp.sum(fresh.reshape(8, 4, -1, 2 * R).astype(F32), axis=0).astype(BF16)
    mine = exchange(jnp.broadcast_to(fresh[None], (8, *fresh.shape)), FAR)
    blocks = (x_own, x_up, x_far, x_down)
    squares = squares_of(blocks)
    mine, x_far, squares = lax.optimization_barrier((mine, x_far, squares))
    mine = mine.reshape(-1, 2 * R)
    weight = exchange(jnp.broadcast_to(mine[None], (8, *mine.shape)), NEAR)
    weight = weight.reshape(8, 8, 4, -1, 2 * R)
    keep, send = project(weight, squares, (x_own, x_up, x_far, x_down))
    return finish(keep, squares, swap(send, 1))[None]


def solution(mesh):
    fine = Mesh(mesh.devices.reshape(4, 2, 2, 2, 2, 4, 2), AXES)
    placed = (
        P(ISLAND, FSDP, TENSOR),
        P(ISLAND, FSDP, None),
        P(ISLAND, FSDP, TENSOR),
        P(FSDP, TENSOR, ISLAND, None),
        P(FSDP, TENSOR, ISLAND, None),
        P(ISLAND, FSDP, TENSOR),
        P(TENSOR),
    )
    return jax.shard_map(
        per_device,
        mesh=fine,
        in_specs=placed,
        out_specs=P(ISLAND, FSDP, TENSOR),
        check_vma=False,
    )
```

```python
import jax
import jax.numpy as jnp
from jax import lax
from jax.experimental import pallas as pl
from jax.experimental.pallas import tpu as pltpu
from jax.sharding import Mesh, PartitionSpec as P

D = 8192
ISLANDS = 8
R = 128
AXES = ("x", "z3", "z2", "z1", "z0", "y", "c")
NEAR = ("x", "z0")
FAR = ("z3", "z2", "z1")
ISLAND = ("x", "z3")
FSDP = ("z2", "z1", "z0")
TENSOR = ("y", "c")
STEP = 0.7 * 1.9
SHARE = STEP / ISLANDS
F32, BF16 = jnp.float32, jnp.bfloat16
VMEM = 16 * 2**20


def exchange(blocks, axes):
    return lax.all_to_all(blocks, axes, 0, 0)


def total(blocks):
    return jnp.sum(blocks.astype(F32), axis=0)


def share_kernel(x_ref, g_ref, w_ref, theta_ref, momentum_ref, gain_ref, out_ref):
    step = pl.program_id(0)
    island, fsdp = lax.axis_index(ISLAND), lax.axis_index(FSDP)
    width = x_ref.shape[1]
    term = lax.dot_general(
        x_ref[...], g_ref[...], (((0,), (0,)), ((), ())), preferred_element_type=F32
    )
    own = (1.0 - STEP) * theta_ref[...] - 0.7 * 0.9 * 0.9 * momentum_ref[...]
    band = []
    for j in range(width // R):
        here = island == step * (width // R) + j
        band.append(SHARE * w_ref[:, j * R : (j + 1) * R].astype(F32) + jnp.where(here, own, 0.0))
    band = jnp.concatenate(band, axis=1).T
    gain = jnp.broadcast_to(gain_ref[...], (R, width)).T
    for j in range(out_ref.shape[1] // R):
        piece = (-0.03 * SHARE) * term[:, j * R : (j + 1) * R]
        piece += jnp.where(fsdp == j, band, 0.0)
        out_ref[:, j * R : (j + 1) * R] = (piece * gain).astype(BF16)


def share(x, g, weight, theta, momentum, gain):
    tokens, features = x.shape
    keys = g.shape[1]
    width = 4 * R
    whole = lambda *shape: pl.BlockSpec(shape, lambda i: (0, 0))
    return pl.pallas_call(
        share_kernel,
        grid=(features // width,),
        in_specs=[
            pl.BlockSpec((tokens, width), lambda i: (0, i)),
            whole(tokens, keys),
            pl.BlockSpec((R, width), lambda i: (0, i)),
            whole(R, R),
            whole(R, R),
            pl.BlockSpec((1, width), lambda i: (0, i)),
        ],
        out_specs=pl.BlockSpec((width, keys), lambda i: (i, 0)),
        out_shape=jax.ShapeDtypeStruct((features, keys), BF16),
        compiler_params=pltpu.CompilerParams(vmem_limit_bytes=60 * 2**20),
        cost_estimate=pl.CostEstimate(
            flops=2 * tokens * features * keys, bytes_accessed=6 * 2**20, transcendentals=0
        ),
    )(x, g, weight, theta, momentum, gain)


def total_kernel(blocks_ref, out_ref):
    for i in range(out_ref.shape[0]):
        rows = slice(i * 16, (i + 1) * 16)
        block = jnp.sum(blocks_ref[:, rows].astype(F32), axis=0).astype(BF16)
        for j in range(4):
            out_ref[i, j] = block[:, j * 2 * R : (j + 1) * 2 * R]


def total_far(blocks):
    return pl.pallas_call(
        total_kernel,
        in_specs=[pl.BlockSpec(memory_space=pltpu.VMEM)],
        out_specs=pl.BlockSpec(memory_space=pltpu.VMEM),
        out_shape=jax.ShapeDtypeStruct((blocks.shape[1] // 16, 4, 16, 2 * R), BF16),
        compiler_params=pltpu.CompilerParams(vmem_limit_bytes=VMEM),
        cost_estimate=pl.CostEstimate(
            flops=blocks.size, bytes_accessed=3 * blocks.size, transcendentals=0
        ),
    )(blocks)


def squares_kernel(*refs):
    x_refs, out_ref = refs[:4], refs[4]

    @pl.loop(0, out_ref.shape[0] // 64)
    def _(i):
        rows = pl.ds(pl.multiple_of(i * 64, 64), 64)
        squares = jnp.zeros((64, R), F32)
        for x_ref in x_refs:
            for j in range(x_ref.shape[1] // R):
                part = x_ref[rows, j * R : (j + 1) * R].astype(F32)
                squares += part * part
        out_ref[rows, :] = jnp.broadcast_to(jnp.sum(squares, axis=1, keepdims=True), (64, R))


def squares_of(blocks):
    tokens, features = blocks[0].shape
    vmem = pl.BlockSpec(memory_space=pltpu.VMEM)
    return pl.pallas_call(
        squares_kernel,
        in_specs=[vmem] * 4,
        out_specs=vmem,
        out_shape=jax.ShapeDtypeStruct((tokens, R), F32),
        compiler_params=pltpu.CompilerParams(vmem_limit_bytes=VMEM),
        cost_estimate=pl.CostEstimate(
            flops=8 * tokens * features, bytes_accessed=8 * tokens * features, transcendentals=0
        ),
    )(*blocks)


def project_kernel(w_ref, squares_ref, *refs):
    x_refs, (keep_ref, send_ref) = refs[:4], refs[4:]
    squares = squares_ref[...]
    own, core = lax.axis_index("y"), lax.axis_index("c")
    tokens = keep_ref.shape[0]
    acc = jnp.zeros((tokens, 2 * R), F32)
    for block, x_ref in enumerate(x_refs):
        acc += jnp.dot(x_ref[...], w_ref[:, :, pl.ds(own ^ block, 1)].reshape(-1, 2 * R), preferred_element_type=F32)
    first = core == 0
    keep_ref[...] = jnp.where(first, acc[:, :R], acc[:, R:])
    high = squares.astype(BF16)
    low = (squares - high.astype(F32)).astype(BF16)
    lane = lax.broadcasted_iota(jnp.int32, (tokens, R), 1)
    send_ref[:, :R] = jnp.where(first, acc[:, R:], acc[:, :R]).astype(BF16)
    send_ref[:, R:] = jnp.where(lane < R // 2, high.astype(F32), low.astype(F32)).astype(BF16)


def project(weight, squares, blocks):
    tokens, features = blocks[0].shape
    vmem = pl.BlockSpec(memory_space=pltpu.VMEM)
    return pl.pallas_call(
        project_kernel,
        in_specs=[vmem] * 6,
        out_specs=(vmem,) * 2,
        out_shape=(
            jax.ShapeDtypeStruct((tokens, R), F32),
            jax.ShapeDtypeStruct((tokens, 2 * R), BF16),
        ),
        compiler_params=pltpu.CompilerParams(vmem_limit_bytes=VMEM),
        cost_estimate=pl.CostEstimate(
            flops=16 * tokens * features * R,
            bytes_accessed=8 * (tokens * features + 2 * features * R),
            transcendentals=0,
        ),
    )(weight, squares, *blocks)


def finish_kernel(keep_ref, squares_ref, got_ref, out_ref):
    other = got_ref[:, R:].astype(F32)
    other = other[:, :1] + other[:, R // 2 : R // 2 + 1]
    scale = lax.rsqrt((squares_ref[...] + other) / D + 1e-05)
    out_ref[...] = ((keep_ref[...] + got_ref[:, :R].astype(F32)) * scale).astype(BF16)


def finish(keep, squares, got):
    vmem = pl.BlockSpec(memory_space=pltpu.VMEM)
    return pl.pallas_call(
        finish_kernel,
        in_specs=[vmem] * 3,
        out_specs=vmem,
        out_shape=jax.ShapeDtypeStruct(keep.shape, BF16),
        compiler_params=pltpu.CompilerParams(vmem_limit_bytes=VMEM),
    )(keep, squares, got)


def swap(block, bits):
    return lax.ppermute(block, TENSOR, [(t, t ^ bits) for t in range(8)])


def per_device(x_saved, grad_keys, inner_weight, outer_weight, outer_momentum, x_next, norm_gain):
    rows, width = outer_weight.shape[0], outer_weight.shape[3]
    term = share(
        x_saved[0],
        grad_keys[0],
        inner_weight[0],
        outer_weight.reshape(rows, width),
        outer_momentum.reshape(rows, width),
        norm_gain[None],
    )
    keys = term.shape[1]
    x_own = x_next[0]
    x_up, x_down, x_far = (swap(x_own, bits) for bits in (2, 6, 4))
    sums = exchange(term.reshape(8, -1, keys), NEAR)
    fresh = exchange(total_far(sums).reshape(32, -1, 2 * R), FAR + ("y",))
    fresh, x_up, x_down = lax.optimization_barrier((fresh, x_up, x_down))
    fresh = jnp.sum(fresh.reshape(8, 4, -1, 2 * R).astype(F32), axis=0).astype(BF16)
    mine = exchange(jnp.broadcast_to(fresh[None], (8, *fresh.shape)), FAR)
    blocks = (x_own, x_up, x_far, x_down)
    squares = squares_of(blocks)
    mine, x_far, squares = lax.optimization_barrier((mine, x_far, squares))
    mine = mine.reshape(-1, 2 * R)
    weight = exchange(jnp.broadcast_to(mine[None], (8, *mine.shape)), NEAR)
    weight = weight.reshape(8, 8, 4, -1, 2 * R)
    keep, send = project(weight, squares, (x_own, x_up, x_far, x_down))
    return finish(keep, squares, swap(send, 1))[None]


def solution(mesh):
    fine = Mesh(mesh.devices.reshape(4, 2, 2, 2, 2, 4, 2), AXES)
    placed = (
        P(ISLAND, FSDP, TENSOR),
        P(ISLAND, FSDP, None),
        P(ISLAND, FSDP, TENSOR),
        P(FSDP, TENSOR, ISLAND, None),
        P(FSDP, TENSOR, ISLAND, None),
        P(ISLAND, FSDP, TENSOR),
        P(TENSOR),
    )
    return jax.shard_map(
        per_device,
        mesh=fine,
        in_specs=placed,
        out_specs=P(ISLAND, FSDP, TENSOR),
        check_vma=False,
    )
```

```python
import jax
import jax.numpy as jnp
from jax import lax
from jax.experimental import pallas as pl
from jax.experimental.pallas import tpu as pltpu
from jax.sharding import Mesh, PartitionSpec as P

D = 8192
ISLANDS = 8
R = 128
AXES = ("x", "z3", "z2", "z1", "z0", "y", "c")
NEAR = ("x", "z0")
FAR = ("z3", "z2", "z1")
ISLAND = ("x", "z3")
FSDP = ("z2", "z1", "z0")
TENSOR = ("y", "c")
STEP = 0.7 * 1.9
SHARE = STEP / ISLANDS
F32, BF16 = jnp.float32, jnp.bfloat16
VMEM = 16 * 2**20


def exchange(blocks, axes):
    return lax.all_to_all(blocks, axes, 0, 0)


def total(blocks):
    return jnp.sum(blocks.astype(F32), axis=0)


def share_kernel(x_ref, g_ref, w_ref, theta_ref, momentum_ref, gain_ref, out_ref, held, sems):
    step = pl.program_id(0)
    island, fsdp = lax.axis_index(ISLAND), lax.axis_index(FSDP)
    width = x_ref.shape[1]
    term = lax.dot_general(
        x_ref[...], g_ref[...], (((0,), (0,)), ((), ())), preferred_element_type=F32
    )
    own = (1.0 - STEP) * theta_ref[...] - 0.7 * 0.9 * 0.9 * momentum_ref[...]
    band = []
    for j in range(width // R):
        here = island == step * (width // R) + j
        band.append(SHARE * w_ref[:, j * R : (j + 1) * R].astype(F32) + jnp.where(here, own, 0.0))
    band = jnp.concatenate(band, axis=1).T
    gain = jnp.broadcast_to(gain_ref[...], (R, width)).T
    chunk = width // 2
    steps = out_ref.shape[0] // width
    copies = []
    for at in range(2 * steps):
        rows = pl.ds(at * chunk, chunk)
        copies.append(pltpu.make_async_copy(held.at[rows], out_ref.at[rows], sems.at[at]))
    for at in range(2):
        rows = slice(at * chunk, (at + 1) * chunk)
        place = pl.ds(pl.multiple_of(step * width + at * chunk, chunk), chunk)
        for j in range(out_ref.shape[1] // R):
            piece = (-0.03 * SHARE) * term[rows, j * R : (j + 1) * R]
            piece += jnp.where(fsdp == j, band[rows], 0.0)
            held[place, j * R : (j + 1) * R] = (piece * gain[rows]).astype(BF16)
        for here in range(steps):

            @pl.when(step == here)
            def _():
                copies[2 * here + at].start()

    @pl.when(step == steps - 1)
    def _():
        for copy in copies:
            copy.wait()


def share(x, g, weight, theta, momentum, gain):
    tokens, features = x.shape
    keys = g.shape[1]
    width = 4 * R
    whole = lambda *shape: pl.BlockSpec(shape, lambda i: (0, 0))
    return pl.pallas_call(
        share_kernel,
        grid=(features // width,),
        in_specs=[
            pl.BlockSpec((tokens, width), lambda i: (0, i)),
            whole(tokens, keys),
            pl.BlockSpec((R, width), lambda i: (0, i)),
            whole(R, R),
            whole(R, R),
            pl.BlockSpec((1, width), lambda i: (0, i)),
        ],
        out_specs=pl.BlockSpec(memory_space=pl.ANY),
        out_shape=jax.ShapeDtypeStruct((features, keys), BF16),
        scratch_shapes=[
            pltpu.VMEM((features, keys), BF16),
            pltpu.SemaphoreType.DMA((2 * features // width,)),
        ],
        compiler_params=pltpu.CompilerParams(vmem_limit_bytes=60 * 2**20),
        cost_estimate=pl.CostEstimate(
            flops=2 * tokens * features * keys, bytes_accessed=6 * 2**20, transcendentals=0
        ),
    )(x, g, weight, theta, momentum, gain)


def total_kernel(blocks_ref, out_ref):
    for i in range(out_ref.shape[0]):
        rows = slice(i * 16, (i + 1) * 16)
        block = jnp.sum(blocks_ref[:, rows].astype(F32), axis=0).astype(BF16)
        for j in range(4):
            out_ref[i, j] = block[:, j * 2 * R : (j + 1) * 2 * R]


def total_far(blocks):
    return pl.pallas_call(
        total_kernel,
        in_specs=[pl.BlockSpec(memory_space=pltpu.VMEM)],
        out_specs=pl.BlockSpec(memory_space=pltpu.VMEM),
        out_shape=jax.ShapeDtypeStruct((blocks.shape[1] // 16, 4, 16, 2 * R), BF16),
        compiler_params=pltpu.CompilerParams(vmem_limit_bytes=VMEM),
        cost_estimate=pl.CostEstimate(
            flops=blocks.size, bytes_accessed=3 * blocks.size, transcendentals=0
        ),
    )(blocks)


def squares_kernel(*refs):
    x_refs, out_ref = refs[:4], refs[4]

    @pl.loop(0, out_ref.shape[0] // 64)
    def _(i):
        rows = pl.ds(pl.multiple_of(i * 64, 64), 64)
        squares = jnp.zeros((64, R), F32)
        for x_ref in x_refs:
            for j in range(x_ref.shape[1] // R):
                part = x_ref[rows, j * R : (j + 1) * R].astype(F32)
                squares += part * part
        out_ref[rows, :] = jnp.broadcast_to(jnp.sum(squares, axis=1, keepdims=True), (64, R))


def squares_of(blocks):
    tokens, features = blocks[0].shape
    vmem = pl.BlockSpec(memory_space=pltpu.VMEM)
    return pl.pallas_call(
        squares_kernel,
        in_specs=[vmem] * 4,
        out_specs=vmem,
        out_shape=jax.ShapeDtypeStruct((tokens, R), F32),
        compiler_params=pltpu.CompilerParams(vmem_limit_bytes=VMEM),
        cost_estimate=pl.CostEstimate(
            flops=8 * tokens * features, bytes_accessed=8 * tokens * features, transcendentals=0
        ),
    )(*blocks)


def project_kernel(w_ref, squares_ref, *refs):
    x_refs, (keep_ref, send_ref) = refs[:4], refs[4:]
    squares = squares_ref[...]
    own, core = lax.axis_index("y"), lax.axis_index("c")
    tokens = keep_ref.shape[0]
    acc = jnp.zeros((tokens, 2 * R), F32)
    for block, x_ref in enumerate(x_refs):
        acc += jnp.dot(x_ref[...], w_ref[:, :, pl.ds(own ^ block, 1)].reshape(-1, 2 * R), preferred_element_type=F32)
    first = core == 0
    keep_ref[...] = jnp.where(first, acc[:, :R], acc[:, R:])
    high = squares.astype(BF16)
    low = (squares - high.astype(F32)).astype(BF16)
    lane = lax.broadcasted_iota(jnp.int32, (tokens, R), 1)
    send_ref[:, :R] = jnp.where(first, acc[:, R:], acc[:, :R]).astype(BF16)
    send_ref[:, R:] = jnp.where(lane < R // 2, high.astype(F32), low.astype(F32)).astype(BF16)


def project(weight, squares, blocks):
    tokens, features = blocks[0].shape
    vmem = pl.BlockSpec(memory_space=pltpu.VMEM)
    return pl.pallas_call(
        project_kernel,
        in_specs=[vmem] * 6,
        out_specs=(vmem,) * 2,
        out_shape=(
            jax.ShapeDtypeStruct((tokens, R), F32),
            jax.ShapeDtypeStruct((tokens, 2 * R), BF16),
        ),
        compiler_params=pltpu.CompilerParams(vmem_limit_bytes=VMEM),
        cost_estimate=pl.CostEstimate(
            flops=16 * tokens * features * R,
            bytes_accessed=8 * (tokens * features + 2 * features * R),
            transcendentals=0,
        ),
    )(weight, squares, *blocks)


def finish_kernel(keep_ref, squares_ref, got_ref, out_ref):
    other = got_ref[:, R:].astype(F32)
    other = other[:, :1] + other[:, R // 2 : R // 2 + 1]
    scale = lax.rsqrt((squares_ref[...] + other) / D + 1e-05)
    out_ref[...] = ((keep_ref[...] + got_ref[:, :R].astype(F32)) * scale).astype(BF16)


def finish(keep, squares, got):
    vmem = pl.BlockSpec(memory_space=pltpu.VMEM)
    return pl.pallas_call(
        finish_kernel,
        in_specs=[vmem] * 3,
        out_specs=vmem,
        out_shape=jax.ShapeDtypeStruct(keep.shape, BF16),
        compiler_params=pltpu.CompilerParams(vmem_limit_bytes=VMEM),
    )(keep, squares, got)


def swap(block, bits):
    return lax.ppermute(block, TENSOR, [(t, t ^ bits) for t in range(8)])


def per_device(x_saved, grad_keys, inner_weight, outer_weight, outer_momentum, x_next, norm_gain):
    rows, width = outer_weight.shape[0], outer_weight.shape[3]
    term = share(
        x_saved[0],
        grad_keys[0],
        inner_weight[0],
        outer_weight.reshape(rows, width),
        outer_momentum.reshape(rows, width),
        norm_gain[None],
    )
    keys = term.shape[1]
    x_own = x_next[0]
    x_up, x_down, x_far = (swap(x_own, bits) for bits in (2, 6, 4))
    sums = exchange(term.reshape(8, -1, keys), NEAR)
    fresh = exchange(total_far(sums).reshape(32, -1, 2 * R), FAR + ("y",))
    fresh, x_up, x_down = lax.optimization_barrier((fresh, x_up, x_down))
    fresh = jnp.sum(fresh.reshape(8, 4, -1, 2 * R).astype(F32), axis=0).astype(BF16)
    mine = exchange(jnp.broadcast_to(fresh[None], (8, *fresh.shape)), FAR)
    blocks = (x_own, x_up, x_far, x_down)
    squares = squares_of(blocks)
    mine, x_far, squares = lax.optimization_barrier((mine, x_far, squares))
    mine = mine.reshape(-1, 2 * R)
    weight = exchange(jnp.broadcast_to(mine[None], (8, *mine.shape)), NEAR)
    weight = weight.reshape(8, 8, 4, -1, 2 * R)
    keep, send = project(weight, squares, (x_own, x_up, x_far, x_down))
    return finish(keep, squares, swap(send, 1))[None]


def solution(mesh):
    fine = Mesh(mesh.devices.reshape(4, 2, 2, 2, 2, 4, 2), AXES)
    placed = (
        P(ISLAND, FSDP, TENSOR),
        P(ISLAND, FSDP, None),
        P(ISLAND, FSDP, TENSOR),
        P(FSDP, TENSOR, ISLAND, None),
        P(FSDP, TENSOR, ISLAND, None),
        P(ISLAND, FSDP, TENSOR),
        P(TENSOR),
    )
    return jax.shard_map(
        per_device,
        mesh=fine,
        in_specs=placed,
        out_specs=P(ISLAND, FSDP, TENSOR),
        check_vma=False,
    )
```

```python
import jax
import jax.numpy as jnp
from jax import lax
from jax.experimental import pallas as pl
from jax.experimental.pallas import tpu as pltpu
from jax.sharding import Mesh, PartitionSpec as P

D = 8192
ISLANDS = 8
R = 128
AXES = ("x", "z3", "z2", "z1", "z0", "y", "c")
NEAR = ("x", "z0")
FAR = ("z3", "z2", "z1")
ISLAND = ("x", "z3")
FSDP = ("z2", "z1", "z0")
TENSOR = ("y", "c")
STEP = 0.7 * 1.9
SHARE = STEP / ISLANDS
F32, BF16 = jnp.float32, jnp.bfloat16
VMEM = 12 * 2**20


def exchange(blocks, axes):
    return lax.all_to_all(blocks, axes, 0, 0)


def total(blocks):
    return jnp.sum(blocks.astype(F32), axis=0)


def share_kernel(x_ref, g_ref, w_ref, theta_ref, momentum_ref, gain_ref, out_ref):
    step = pl.program_id(0)
    island, fsdp = lax.axis_index(ISLAND), lax.axis_index(FSDP)
    width = x_ref.shape[1]
    term = lax.dot_general(
        x_ref[...], g_ref[...], (((0,), (0,)), ((), ())), preferred_element_type=F32
    )
    own = (1.0 - STEP) * theta_ref[...] - 0.7 * 0.9 * 0.9 * momentum_ref[...]
    band = []
    for j in range(width // R):
        here = island == step * (width // R) + j
        band.append(SHARE * w_ref[:, j * R : (j + 1) * R].astype(F32) + jnp.where(here, own, 0.0))
    band = jnp.concatenate(band, axis=1).T
    gain = jnp.broadcast_to(gain_ref[...], (R, width)).T
    for j in range(out_ref.shape[1] // R):
        piece = (-0.03 * SHARE) * term[:, j * R : (j + 1) * R]
        piece += jnp.where(fsdp == j, band, 0.0)
        out_ref[:, j * R : (j + 1) * R] = (piece * gain).astype(BF16)


def share(x, g, weight, theta, momentum, gain):
    tokens, features = x.shape
    keys = g.shape[1]
    width = 4 * R
    whole = lambda *shape: pl.BlockSpec(shape, lambda i: (0, 0))
    return pl.pallas_call(
        share_kernel,
        grid=(features // width,),
        in_specs=[
            pl.BlockSpec((tokens, width), lambda i: (0, i)),
            whole(tokens, keys),
            pl.BlockSpec((R, width), lambda i: (0, i)),
            whole(R, R),
            whole(R, R),
            pl.BlockSpec((1, width), lambda i: (0, i)),
        ],
        out_specs=pl.BlockSpec((width, keys), lambda i: (i, 0)),
        out_shape=jax.ShapeDtypeStruct((features, keys), BF16),
        compiler_params=pltpu.CompilerParams(vmem_limit_bytes=60 * 2**20),
        cost_estimate=pl.CostEstimate(
            flops=2 * tokens * features * keys, bytes_accessed=6 * 2**20, transcendentals=0
        ),
    )(x, g, weight, theta, momentum, gain)


def total_kernel(blocks_ref, out_ref):
    for i in range(out_ref.shape[0]):
        rows = slice(i * 16, (i + 1) * 16)
        block = jnp.sum(blocks_ref[:, rows].astype(F32), axis=0).astype(BF16)
        for j in range(4):
            out_ref[i, j] = block[:, j * 2 * R : (j + 1) * 2 * R]


def total_far(blocks):
    return pl.pallas_call(
        total_kernel,
        in_specs=[pl.BlockSpec(memory_space=pltpu.VMEM)],
        out_specs=pl.BlockSpec(memory_space=pltpu.VMEM),
        out_shape=jax.ShapeDtypeStruct((blocks.shape[1] // 16, 4, 16, 2 * R), BF16),
        compiler_params=pltpu.CompilerParams(vmem_limit_bytes=VMEM),
        cost_estimate=pl.CostEstimate(
            flops=blocks.size, bytes_accessed=3 * blocks.size, transcendentals=0
        ),
    )(blocks)


def squares_kernel(*refs):
    x_refs, out_ref = refs[:4], refs[4]

    @pl.loop(0, out_ref.shape[0] // 64)
    def _(i):
        rows = pl.ds(pl.multiple_of(i * 64, 64), 64)
        squares = jnp.zeros((64, R), F32)
        for x_ref in x_refs:
            for j in range(x_ref.shape[1] // R):
                part = x_ref[rows, j * R : (j + 1) * R].astype(F32)
                squares += part * part
        out_ref[rows, :] = jnp.broadcast_to(jnp.sum(squares, axis=1, keepdims=True), (64, R))


def squares_of(blocks):
    tokens, features = blocks[0].shape
    vmem = pl.BlockSpec(memory_space=pltpu.VMEM)
    return pl.pallas_call(
        squares_kernel,
        in_specs=[vmem] * 4,
        out_specs=vmem,
        out_shape=jax.ShapeDtypeStruct((tokens, R), F32),
        compiler_params=pltpu.CompilerParams(vmem_limit_bytes=VMEM),
        cost_estimate=pl.CostEstimate(
            flops=8 * tokens * features, bytes_accessed=8 * tokens * features, transcendentals=0
        ),
    )(*blocks)


def project_kernel(w_ref, squares_ref, *refs):
    x_refs, (keep_ref, send_ref) = refs[:4], refs[4:]
    squares = squares_ref[...]
    own, core = lax.axis_index("y"), lax.axis_index("c")
    tokens = keep_ref.shape[0]
    acc = jnp.zeros((tokens, 2 * R), F32)
    for block, x_ref in enumerate(x_refs):
        acc += jnp.dot(x_ref[...], w_ref[:, :, pl.ds(own ^ block, 1)].reshape(-1, 2 * R), preferred_element_type=F32)
    first = core == 0
    keep_ref[...] = jnp.where(first, acc[:, :R], acc[:, R:])
    high = squares.astype(BF16)
    low = (squares - high.astype(F32)).astype(BF16)
    lane = lax.broadcasted_iota(jnp.int32, (tokens, R), 1)
    send_ref[:, :R] = jnp.where(first, acc[:, R:], acc[:, :R]).astype(BF16)
    send_ref[:, R:] = jnp.where(lane < R // 2, high.astype(F32), low.astype(F32)).astype(BF16)


def project(weight, squares, blocks):
    tokens, features = blocks[0].shape
    vmem = pl.BlockSpec(memory_space=pltpu.VMEM)
    return pl.pallas_call(
        project_kernel,
        in_specs=[vmem] * 6,
        out_specs=(vmem,) * 2,
        out_shape=(
            jax.ShapeDtypeStruct((tokens, R), F32),
            jax.ShapeDtypeStruct((tokens, 2 * R), BF16),
        ),
        compiler_params=pltpu.CompilerParams(vmem_limit_bytes=VMEM),
        cost_estimate=pl.CostEstimate(
            flops=16 * tokens * features * R,
            bytes_accessed=8 * (tokens * features + 2 * features * R),
            transcendentals=0,
        ),
    )(weight, squares, *blocks)


def finish_kernel(keep_ref, squares_ref, got_ref, out_ref):
    other = got_ref[:, R:].astype(F32)
    other = other[:, :1] + other[:, R // 2 : R // 2 + 1]
    scale = lax.rsqrt((squares_ref[...] + other) / D + 1e-05)
    out_ref[...] = ((keep_ref[...] + got_ref[:, :R].astype(F32)) * scale).astype(BF16)


def finish(keep, squares, got):
    vmem = pl.BlockSpec(memory_space=pltpu.VMEM)
    return pl.pallas_call(
        finish_kernel,
        in_specs=[vmem] * 3,
        out_specs=vmem,
        out_shape=jax.ShapeDtypeStruct(keep.shape, BF16),
        compiler_params=pltpu.CompilerParams(vmem_limit_bytes=VMEM),
    )(keep, squares, got)


def swap(block, bits):
    return lax.ppermute(block, TENSOR, [(t, t ^ bits) for t in range(8)])


def per_device(x_saved, grad_keys, inner_weight, outer_weight, outer_momentum, x_next, norm_gain):
    rows, width = outer_weight.shape[0], outer_weight.shape[3]
    term = share(
        x_saved[0],
        grad_keys[0],
        inner_weight[0],
        outer_weight.reshape(rows, width),
        outer_momentum.reshape(rows, width),
        norm_gain[None],
    )
    keys = term.shape[1]
    x_own = x_next[0]
    x_up, x_down, x_far = (swap(x_own, bits) for bits in (2, 6, 4))
    sums = exchange(term.reshape(8, -1, keys), NEAR)
    fresh = exchange(total_far(sums).reshape(32, -1, 2 * R), FAR + ("y",))
    fresh, x_far = lax.optimization_barrier((fresh, x_far))
    fresh = jnp.sum(fresh.reshape(8, 4, -1, 2 * R).astype(F32), axis=0).astype(BF16)
    mine = exchange(jnp.broadcast_to(fresh[None], (8, *fresh.shape)), FAR)
    blocks = (x_own, x_up, x_far, x_down)
    squares = squares_of(blocks)
    mine, squares = lax.optimization_barrier((mine, squares))
    mine = mine.reshape(-1, 2 * R)
    weight = exchange(jnp.broadcast_to(mine[None], (8, *mine.shape)), NEAR)
    weight = weight.reshape(8, 8, 4, -1, 2 * R)
    keep, send = project(weight, squares, (x_own, x_up, x_far, x_down))
    return finish(keep, squares, swap(send, 1))[None]


def solution(mesh):
    fine = Mesh(mesh.devices.reshape(4, 2, 2, 2, 2, 4, 2), AXES)
    placed = (
        P(ISLAND, FSDP, TENSOR),
        P(ISLAND, FSDP, None),
        P(ISLAND, FSDP, TENSOR),
        P(FSDP, TENSOR, ISLAND, None),
        P(FSDP, TENSOR, ISLAND, None),
        P(ISLAND, FSDP, TENSOR),
        P(TENSOR),
    )
    return jax.shard_map(
        per_device,
        mesh=fine,
        in_specs=placed,
        out_specs=P(ISLAND, FSDP, TENSOR),
        check_vma=False,
    )
```

```python
import jax
import jax.numpy as jnp
from jax import lax
from jax.experimental import pallas as pl
from jax.experimental.pallas import tpu as pltpu
from jax.sharding import Mesh, PartitionSpec as P

D = 8192
ISLANDS = 8
R = 128
AXES = ("x", "z3", "z2", "z1", "z0", "y", "c")
NEAR = ("x", "z0")
FAR = ("z3", "z2", "z1")
ISLAND = ("x", "z3")
FSDP = ("z2", "z1", "z0")
TENSOR = ("y", "c")
STEP = 0.7 * 1.9
SHARE = STEP / ISLANDS
F32, BF16 = jnp.float32, jnp.bfloat16
VMEM = 16 * 2**20


def exchange(blocks, axes):
    return lax.all_to_all(blocks, axes, 0, 0)


def total(blocks):
    return jnp.sum(blocks.astype(F32), axis=0)


def share_kernel(x_ref, g_ref, w_ref, theta_ref, momentum_ref, gain_ref, out_ref):
    step = pl.program_id(0)
    island, fsdp = lax.axis_index(ISLAND), lax.axis_index(FSDP)
    width = x_ref.shape[1]
    term = lax.dot_general(
        x_ref[...], g_ref[...], (((0,), (0,)), ((), ())), preferred_element_type=F32
    )
    own = (1.0 - STEP) * theta_ref[...] - 0.7 * 0.9 * 0.9 * momentum_ref[...]
    band = []
    for j in range(width // R):
        here = island == step * (width // R) + j
        band.append(SHARE * w_ref[:, j * R : (j + 1) * R].astype(F32) + jnp.where(here, own, 0.0))
    band = jnp.concatenate(band, axis=1).T
    gain = jnp.broadcast_to(gain_ref[...], (R, width)).T
    for j in range(out_ref.shape[1] // R):
        piece = (-0.03 * SHARE) * term[:, j * R : (j + 1) * R]
        piece += jnp.where(fsdp == j, band, 0.0)
        out_ref[:, j * R : (j + 1) * R] = (piece * gain).astype(BF16)


def share(x, g, weight, theta, momentum, gain):
    tokens, features = x.shape
    keys = g.shape[1]
    width = 4 * R
    whole = lambda *shape: pl.BlockSpec(shape, lambda i: (0, 0))
    return pl.pallas_call(
        share_kernel,
        grid=(features // width,),
        in_specs=[
            pl.BlockSpec((tokens, width), lambda i: (0, i)),
            whole(tokens, keys),
            pl.BlockSpec((R, width), lambda i: (0, i)),
            whole(R, R),
            whole(R, R),
            pl.BlockSpec((1, width), lambda i: (0, i)),
        ],
        out_specs=pl.BlockSpec((width, keys), lambda i: (i, 0)),
        out_shape=jax.ShapeDtypeStruct((features, keys), BF16),
        compiler_params=pltpu.CompilerParams(vmem_limit_bytes=60 * 2**20),
        cost_estimate=pl.CostEstimate(
            flops=2 * tokens * features * keys, bytes_accessed=6 * 2**20, transcendentals=0
        ),
    )(x, g, weight, theta, momentum, gain)


def total_kernel(blocks_ref, out_ref):
    for i in range(out_ref.shape[0]):
        rows = slice(i * 16, (i + 1) * 16)
        block = jnp.sum(blocks_ref[:, rows].astype(F32), axis=0).astype(BF16)
        for j in range(4):
            out_ref[i, j] = block[:, j * 2 * R : (j + 1) * 2 * R]


def total_far(blocks):
    return pl.pallas_call(
        total_kernel,
        in_specs=[pl.BlockSpec(memory_space=pltpu.VMEM)],
        out_specs=pl.BlockSpec(memory_space=pltpu.VMEM),
        out_shape=jax.ShapeDtypeStruct((blocks.shape[1] // 16, 4, 16, 2 * R), BF16),
        compiler_params=pltpu.CompilerParams(vmem_limit_bytes=VMEM),
        cost_estimate=pl.CostEstimate(
            flops=blocks.size, bytes_accessed=3 * blocks.size, transcendentals=0
        ),
    )(blocks)


def squares_kernel(*refs):
    x_refs, out_ref = refs[:4], refs[4]

    @pl.loop(0, out_ref.shape[0] // 64)
    def _(i):
        rows = pl.ds(pl.multiple_of(i * 64, 64), 64)
        squares = jnp.zeros((64, R), F32)
        for x_ref in x_refs:
            for j in range(x_ref.shape[1] // R):
                part = x_ref[rows, j * R : (j + 1) * R].astype(F32)
                squares += part * part
        out_ref[rows, :] = jnp.broadcast_to(jnp.sum(squares, axis=1, keepdims=True), (64, R))


def squares_of(blocks):
    tokens, features = blocks[0].shape
    vmem = pl.BlockSpec(memory_space=pltpu.VMEM)
    return pl.pallas_call(
        squares_kernel,
        in_specs=[vmem] * 4,
        out_specs=vmem,
        out_shape=jax.ShapeDtypeStruct((tokens, R), F32),
        compiler_params=pltpu.CompilerParams(vmem_limit_bytes=VMEM),
        cost_estimate=pl.CostEstimate(
            flops=8 * tokens * features, bytes_accessed=8 * tokens * features, transcendentals=0
        ),
    )(*blocks)


def project_kernel(w_ref, squares_ref, *refs):
    x_refs, (keep_ref, send_ref) = refs[:4], refs[4:]
    squares = squares_ref[...]
    own, core = lax.axis_index("y"), lax.axis_index("c")
    tokens = keep_ref.shape[0]
    acc = jnp.zeros((tokens, 2 * R), F32)
    for block, x_ref in enumerate(x_refs):
        acc += jnp.dot(x_ref[...], w_ref[:, :, pl.ds(own ^ block, 1)].reshape(-1, 2 * R), preferred_element_type=F32)
    first = core == 0
    keep_ref[...] = jnp.where(first, acc[:, :R], acc[:, R:])
    high = squares.astype(BF16)
    low = (squares - high.astype(F32)).astype(BF16)
    lane = lax.broadcasted_iota(jnp.int32, (tokens, R), 1)
    send_ref[:, :R] = jnp.where(first, acc[:, R:], acc[:, :R]).astype(BF16)
    send_ref[:, R:] = jnp.where(lane < R // 2, high.astype(F32), low.astype(F32)).astype(BF16)


def project(weight, squares, blocks):
    tokens, features = blocks[0].shape
    vmem = pl.BlockSpec(memory_space=pltpu.VMEM)
    return pl.pallas_call(
        project_kernel,
        in_specs=[vmem] * 6,
        out_specs=(vmem,) * 2,
        out_shape=(
            jax.ShapeDtypeStruct((tokens, R), F32),
            jax.ShapeDtypeStruct((tokens, 2 * R), BF16),
        ),
        compiler_params=pltpu.CompilerParams(vmem_limit_bytes=VMEM),
        cost_estimate=pl.CostEstimate(
            flops=16 * tokens * features * R,
            bytes_accessed=8 * (tokens * features + 2 * features * R),
            transcendentals=0,
        ),
    )(weight, squares, *blocks)


def finish_kernel(keep_ref, squares_ref, got_ref, out_ref):
    other = got_ref[:, R:].astype(F32)
    other = other[:, :1] + other[:, R // 2 : R // 2 + 1]
    scale = lax.rsqrt((squares_ref[...] + other) / D + 1e-05)
    out_ref[...] = ((keep_ref[...] + got_ref[:, :R].astype(F32)) * scale).astype(BF16)


def finish(keep, squares, got):
    vmem = pl.BlockSpec(memory_space=pltpu.VMEM)
    return pl.pallas_call(
        finish_kernel,
        in_specs=[vmem] * 3,
        out_specs=vmem,
        out_shape=jax.ShapeDtypeStruct(keep.shape, BF16),
        compiler_params=pltpu.CompilerParams(vmem_limit_bytes=VMEM),
    )(keep, squares, got)


def swap(block, bits):
    return lax.ppermute(block, TENSOR, [(t, t ^ bits) for t in range(8)])


def per_device(x_saved, grad_keys, inner_weight, outer_weight, outer_momentum, x_next, norm_gain):
    rows, width = outer_weight.shape[0], outer_weight.shape[3]
    term = share(
        x_saved[0],
        grad_keys[0],
        inner_weight[0],
        outer_weight.reshape(rows, width),
        outer_momentum.reshape(rows, width),
        norm_gain[None],
    )
    keys = term.shape[1]
    x_own = x_next[0]
    x_up, x_down, x_far = (swap(x_own, bits) for bits in (2, 6, 4))
    sums = exchange(term.reshape(8, -1, keys), NEAR)
    fresh = exchange(total_far(sums).reshape(32, -1, 2 * R), FAR + ("y",))
    fresh, x_up, x_down = lax.optimization_barrier((fresh, x_up, x_down))
    fresh = jnp.sum(fresh.reshape(8, 4, -1, 2 * R).astype(F32), axis=0).astype(BF16)
    mine = exchange(jnp.broadcast_to(fresh[None], (8, *fresh.shape)), FAR)
    blocks = (x_own, x_up, x_far, x_down)
    squares = squares_of(blocks)
    mine, x_far, squares = lax.optimization_barrier((mine, x_far, squares))
    mine = mine.reshape(-1, 2 * R)
    weight = exchange(jnp.broadcast_to(mine[None], (8, *mine.shape)), NEAR)
    weight = weight.reshape(8, 8, 4, -1, 2 * R)
    keep, send = project(weight, squares, (x_own, x_up, x_far, x_down))
    got = swap(send, 1).astype(F32)
    scale = lax.rsqrt((squares[:, :1] + got[:, R : R + 1] + got[:, -1:]) / D + 1e-05)
    return ((keep + got[:, :R]) * scale).astype(BF16)[None]


def solution(mesh):
    fine = Mesh(mesh.devices.reshape(4, 2, 2, 2, 2, 4, 2), AXES)
    placed = (
        P(ISLAND, FSDP, TENSOR),
        P(ISLAND, FSDP, None),
        P(ISLAND, FSDP, TENSOR),
        P(FSDP, TENSOR, ISLAND, None),
        P(FSDP, TENSOR, ISLAND, None),
        P(ISLAND, FSDP, TENSOR),
        P(TENSOR),
    )
    return jax.shard_map(
        per_device,
        mesh=fine,
        in_specs=placed,
        out_specs=P(ISLAND, FSDP, TENSOR),
        check_vma=False,
    )
```
